128 devices in a mesh: row: 8 (over z_lo, x), col: 16 (over y, z_hi, core).
Axes of the slice: x: 4, y: 4, z: 4 (z_hi: 2, z_lo: 2; z = z_hi * 2 + z_lo), core: 2. Of those that a mesh axis runs over, the one named last changes fastest.
Arguments:
- tokens_map: bfloat16 [512, 1024, 384], P('row', 'col'), may hold values from -6 to 6
- gain_attn: float32 [384], replicated, may hold values from 0.1 to 1.9
- w_qkv: bfloat16 [384, 1152], replicated, may hold values from -1 to 1
- w_proj: bfloat16 [384, 384], replicated, may hold values from -0.3125 to 0.3125
- rel_bias: float32 [12, 15, 15], replicated, may hold values from -4 to 4
- gain_mlp: float32 [384], replicated, may hold values from 0.1 to 1.9
- w_up: bfloat16 [384, 1536], replicated, may hold values from -0.3125 to 0.3125
- w_down: bfloat16 [1536, 384], replicated, may hold values from -0.15625 to 0.15625
Outputs:
- block_out: bfloat16 [512, 1024, 384], P('row', 'col')
The draws below stay inside these ranges and needn't reach their ends.
All inputs are finite; a program needn't handle non-finite values.
Results may differ from the reference program's by a relative error of at most 0.0062.
Values may be sent and summed in bfloat16 or wider, within the bound.
A program may use at most 192 MiB of HBM per device.

```python
import jax
import jax.numpy as jnp
from jax import lax

D = 384
HEADS = 12
HEAD_DIM = 32
MLP_DIM = 1536
GRID = 8
ROWS = 512
COLS = 1024


def draw_w_qkv(key, part):
    key = jax.random.fold_in(key, 11)
    entries = jax.random.normal(jax.random.fold_in(key, 1), (D, 3 * D), jnp.float32) / D ** 0.5
    return jnp.clip(entries, -1.0, 1.0).astype(jnp.bfloat16)


def block_levels(key, dims, shards, smallest, top_value):
    def one(axis_at, blocks):
        draws = jax.random.uniform(jax.random.fold_in(jax.random.fold_in(key, 6), axis_at), (blocks,), jnp.float32, smallest / len(shards), top_value / len(shards))
        return jnp.repeat(jnp.exp(draws), dims[axis_at] // blocks).reshape((-1,) + (1,) * (len(dims) - axis_at - 1))

    gain = one(*shards[0])
    for cut in shards[1:]:
        gain = gain * one(*cut)
    return gain


def normal_values(own_key, extent, scale, most, split=(), kind=jnp.bfloat16):
    result = jax.random.normal(own_key, extent, jnp.float32) * scale
    if len(split) > 0:
        result = block_levels(own_key, extent, split, -0.22, 0.18) * result
    return jnp.clip(result, min=-most, max=most).astype(kind)


def setup_inputs(seed: int = 0) -> dict:
    arg_keys = jax.random.split(jax.random.key(seed), 9)
    tokens_map = normal_values(arg_keys[0], (ROWS, COLS, D), 1.0, 6.0, ((0, 8), (1, 16)))
    gain_attn = jnp.clip(1.0 + 0.18 * jax.random.normal(arg_keys[1], (D,), jnp.float32), 0.1, 1.9)
    w_qkv = draw_w_qkv(jax.random.fold_in(arg_keys[8], 71), 0)
    w_proj = normal_values(arg_keys[3], (D, D), D ** -0.5, 0.3125)
    rel_bias = normal_values(arg_keys[4], (HEADS, 2 * GRID - 1, 2 * GRID - 1), 1.0, 4.0, (), jnp.float32)
    gain_mlp = jnp.clip(1.0 + 0.18 * jax.random.normal(arg_keys[5], (D,), jnp.float32), 0.1, 1.9)
    w_up = normal_values(arg_keys[6], (D, MLP_DIM), D ** -0.5, 0.3125)
    w_down = normal_values(arg_keys[7], (MLP_DIM, D), MLP_DIM ** -0.5, 0.15625)
    return dict(tokens_map=tokens_map, gain_attn=gain_attn, w_qkv=w_qkv, w_proj=w_proj, rel_bias=rel_bias, gain_mlp=gain_mlp, w_up=w_up, w_down=w_down)


epsilon = 1e-05

def layer_norm(inputs, gain_vector):
    values = inputs.astype(jnp.float32)
    average = lax.optimization_barrier(jnp.mean(values, -1, keepdims=True))
    centered = values - average
    variance = lax.optimization_barrier(jnp.mean(centered * centered, -1, keepdims=True))
    return (centered * lax.rsqrt(variance + epsilon) * gain_vector).astype(jnp.bfloat16)

def pair_bias(rel_bias):
    places = jnp.arange(GRID * GRID, dtype=jnp.int32)
    row_of = places // GRID
    col_of = places % GRID
    offsets = jnp.arange(2 * GRID - 1, dtype=jnp.int32)
    row_hits = (row_of[:, None, None] - row_of[None, :, None] + GRID - 1 == offsets).astype(jnp.float32)
    col_hits = (col_of[:, None, None] - col_of[None, :, None] + GRID - 1 == offsets).astype(jnp.float32)
    return jnp.einsum('ijp,hpq,ijq->hij', row_hits, rel_bias.astype(jnp.float32), col_hits, precision=lax.Precision.HIGHEST)

def attend(groups, gain_attn, w_qkv, w_proj, bias_full):
    group_count = groups.shape[0]
    members = GRID * GRID
    normed = layer_norm(groups.reshape(group_count * members, D), gain_attn)
    packed = jnp.dot(normed, w_qkv, preferred_element_type=jnp.float32).astype(jnp.bfloat16)
    packed = packed.reshape(group_count, members, 3, HEADS, HEAD_DIM)
    query_heads = packed[:, :, 0].astype(jnp.float32)
    key_heads = packed[:, :, 1].astype(jnp.float32)
    value_heads = packed[:, :, 2].astype(jnp.float32)
    scores = jnp.einsum('gihe,gjhe->ghij', query_heads, key_heads) * HEAD_DIM ** (-0.5) + bias_full[None]
    row_peak = lax.optimization_barrier(jnp.max(scores, -1, keepdims=True))
    weights = jnp.exp(scores - row_peak)
    probabilities = (weights / lax.optimization_barrier(jnp.sum(weights, -1, keepdims=True))).astype(jnp.bfloat16)
    mixture = jnp.einsum('ghij,gjhe->gihe', probabilities.astype(jnp.float32), value_heads).astype(jnp.bfloat16)
    mixture = mixture.reshape(group_count * members, D)
    attended = groups.reshape(group_count * members, D).astype(jnp.float32) + jnp.dot(mixture, w_proj, preferred_element_type=jnp.float32)
    return attended.astype(jnp.bfloat16).reshape(group_count, members, D)

def mlp_part(token_rows, gain_mlp, w_up, w_down):
    normed = layer_norm(token_rows, gain_mlp)
    hidden_units = jax.nn.gelu(jnp.dot(normed, w_up, preferred_element_type=jnp.float32), approximate=False).astype(jnp.bfloat16)
    return (token_rows.astype(jnp.float32) + jnp.dot(hidden_units, w_down, preferred_element_type=jnp.float32)).astype(jnp.bfloat16)

def reference(tokens_map, gain_attn, w_qkv, w_proj, rel_bias, gain_mlp, w_up, w_down):
    bias_full = pair_bias(rel_bias)
    stride_rows = ROWS // GRID
    stride_cols = COLS // GRID
    arranged = tokens_map.reshape(GRID, stride_rows, GRID, stride_cols, D).transpose(1, 3, 0, 2, 4)
    arranged = arranged.reshape(stride_rows, stride_cols, GRID * GRID, D)

    def one_slab(slab_rows):
        attended = attend(slab_rows, gain_attn, w_qkv, w_proj, bias_full)
        finished = mlp_part(attended.reshape(stride_cols * GRID * GRID, D), gain_mlp, w_up, w_down)
        return finished.reshape(stride_cols, GRID * GRID, D)
    results = lax.map(one_slab, arranged)
    results = results.reshape(stride_rows, stride_cols, GRID, GRID, D).transpose(2, 0, 3, 1, 4)
    return results.reshape(ROWS, COLS, D)
```

```python
import math

import jax
import jax.numpy as jnp
from jax import lax
from jax.experimental import pallas as pl
from jax.experimental.pallas import tpu as pltpu
from jax.sharding import PartitionSpec as P

MESH = pl.DeviceIdType.MESH
f32, bf16 = jnp.float32, jnp.bfloat16

D = 384
HEADS = 12
HEAD_DIM = 32
MLP_DIM = 1536
GRID = 8
MEMBERS = GRID * GRID
EPSILON = 1e-5
LOG2E = math.log2(math.e)

CHUNK = 16
TILE = 16
CHUNKS = 4
ATTN_TILES = 4
MLP_TILES = 2


def norm(values, gain):
    average = jnp.mean(values, -1, keepdims=True)
    centered = values - average
    variance = jnp.mean(centered * centered, -1, keepdims=True)
    return (centered * lax.rsqrt(variance + EPSILON) * gain).astype(bf16)


def fill_swap(swap):
    r = lax.broadcasted_iota(jnp.int32, (256, 256), 0)
    c = lax.broadcasted_iota(jnp.int32, (256, 256), 1)
    swap[...] = ((r // 16 == c % 16) & (r % 16 == c // 16)).astype(bf16)


def fill_ones(ones):
    r = lax.broadcasted_iota(jnp.int32, (256, 128), 0)
    c = lax.broadcasted_iota(jnp.int32, (256, 128), 1)
    ones[...] = (r // MEMBERS == c // HEAD_DIM).astype(bf16)


def fill_bias(rel, strip, bias):
    s = lax.broadcasted_iota(jnp.int32, (15, 1024), 0)
    lane = lax.broadcasted_iota(jnp.int32, (15, 1024), 1)
    g2i, q, g2j = lane // 128, (lane % 128) // 8, lane % 8
    hits = ((s == g2i - g2j + 7) & (q < 15)).astype(f32)
    rows = s == 14 - q
    for h in range(HEADS):
        spread = jnp.dot(rel[h], hits, preferred_element_type=f32, precision=lax.Precision.HIGHEST)
        line = jnp.sum(jnp.where(rows, spread, 0.0), 0, keepdims=True) * LOG2E
        for g in range(GRID):
            strip[h, g:g + 1, :] = line[:, g * 128:(g + 1) * 128]
    for h in range(HEADS):
        u = strip[h]
        for g1 in range(GRID):
            at = (GRID - 1 - g1) * GRID
            lanes = slice((h % 4) * MEMBERS, (h % 4 + 1) * MEMBERS)
            bias[h // 4, g1 * GRID:(g1 + 1) * GRID, lanes] = u[:, at:at + MEMBERS]


def turn(swap, rows):
    parts = [
        jnp.dot(swap, rows[at:at + 256], preferred_element_type=f32).astype(bf16)
        for at in range(0, rows.shape[0], 256)
    ]
    return parts[0] if len(parts) == 1 else jnp.concatenate(parts, 0)


def project(step, tokens, gain, w_qkv, swap, qkv):
    first = step * ATTN_TILES * TILE
    x = tokens[pl.ds(first, ATTN_TILES * TILE)].reshape(ATTN_TILES * 256, D).astype(f32)
    turned = turn(swap[...], norm(x, gain))
    packed = jnp.dot(turned, w_qkv[...], preferred_element_type=f32).astype(bf16)
    for part in range(3):
        for t in range(ATTN_TILES):
            block = packed[t * 256:(t + 1) * 256, part * D:(part + 1) * D]
            qkv[part, :, pl.ds(first + t * TILE, TILE), :] = block.reshape(CHUNK, TILE, D)


def attend(b, qkv, bias, ones, mix):
    lane = lax.broadcasted_iota(jnp.int32, (1, 128), 1)
    low = lane < MEMBERS
    masks = [(lane // HEAD_DIM == h).astype(bf16) for h in range(4)]
    for hb in range(3):
        cols = slice(hb * 128, (hb + 1) * 128)
        q = qkv[0, b, :, cols]
        k = qkv[1, b, :, cols]
        v = qkv[2, b, :, cols]
        keys = jnp.concatenate([k * m for m in masks], 0)
        values = jnp.concatenate([v * m for m in masks], 0)
        scores = lax.dot_general(q, keys, (((1,), (1,)), ((), ())), preferred_element_type=f32)
        scores = scores * (HEAD_DIM ** -0.5 * LOG2E) + bias[hb]
        weights = []
        for pair in range(2):
            s = scores[:, pair * 128:(pair + 1) * 128]
            peak0 = jnp.max(jnp.where(low, s, -jnp.inf), -1, keepdims=True)
            peak1 = jnp.max(jnp.where(low, -jnp.inf, s), -1, keepdims=True)
            weights.append(jnp.exp2(s - jnp.where(low, peak0, peak1)).astype(bf16))
        sums = jnp.dot(
            jnp.concatenate(weights, 1),
            jnp.concatenate([values, ones[...]], 1),
            preferred_element_type=f32,
        )
        mixture = (sums[:, :128] / sums[:, 128:]).astype(bf16)
        mix[:, pl.ds(b, 1), :, cols] = mixture.reshape(MEMBERS // TILE, 1, TILE, 128)


def finish(step, tokens, mix, swap, w_proj, gain, w_up, w_down, done):
    rows = MLP_TILES * 256
    first = step * MLP_TILES * TILE
    x = tokens[pl.ds(first, MLP_TILES * TILE)].reshape(rows, D).astype(f32)
    mixture = turn(swap[...], mix[pl.ds(step * MLP_TILES, MLP_TILES)].reshape(rows, D))
    attended = (x + jnp.dot(mixture, w_proj[...], preferred_element_type=f32)).astype(bf16)
    normed = norm(attended.astype(f32), gain)
    hidden = []
    for c in range(0, MLP_DIM, 512):
        u = jnp.dot(normed, w_up[:, c:c + 512], preferred_element_type=f32)
        hidden.append((u * (0.5 * lax.erf(u * (2 ** -0.5)) + 0.5)).astype(bf16))
    total = attended.astype(f32) + jnp.dot(
        jnp.concatenate(hidden, 1), w_down[...], preferred_element_type=f32
    )
    done[pl.ds(first, MLP_TILES * TILE)] = total.astype(bf16).reshape(MLP_TILES * TILE, CHUNK, D)


def kernel(
    x_ref, gain_attn, wq_ref, wp_ref, rel, gain_mlp, wu_ref, wd_ref,
    out_ref,
    tokens, done, w_qkv, w_proj, w_up, w_down, qkv, mix, bias, strip, swap, ones,
    weight_sem, in_sem, sent_sem, back_sem, out_sem,
):
    g1 = lax.axis_index("row")
    col = lax.axis_index("col")
    g2, core = col // 2, col % 2
    me = g1 * GRID + g2

    def partner(t):
        p1, p2 = lax.rem(g1 + t // GRID, GRID), lax.rem(g2 + lax.rem(t, GRID), GRID)
        return p1 * GRID + p2, (p1, p2 * 2 + core)

    barrier = pltpu.get_barrier_semaphore()

    @pl.loop(1, MEMBERS)
    def _(t):
        pl.semaphore_signal(barrier, inc=1, device_id=partner(t)[1], device_id_type=MESH)

    weights = [
        pltpu.make_async_copy(src, dst, weight_sem.at[i])
        for i, (src, dst) in enumerate(
            ((wq_ref, w_qkv), (wp_ref, w_proj), (wu_ref, w_up), (wd_ref, w_down))
        )
    ]
    for c in range(CHUNKS):
        pltpu.make_async_copy(
            x_ref.at[me, pl.ds(c * CHUNK, CHUNK)], tokens.at[c, me], in_sem.at[c]
        ).start()
    for copy in weights:
        copy.start()
    pl.semaphore_wait(barrier, MEMBERS - 1)

    for c in range(CHUNKS):

        @pl.loop(1, MEMBERS)
        def _(t):
            peer, device = partner(t)
            pltpu.make_async_remote_copy(
                src_ref=x_ref.at[peer, pl.ds(c * CHUNK, CHUNK)],
                dst_ref=tokens.at[c, me],
                send_sem=sent_sem.at[0],
                recv_sem=in_sem.at[c],
                device_id=device,
                device_id_type=MESH,
            ).start()

    fill_swap(swap)
    fill_ones(ones)
    fill_bias(rel, strip, bias)
    for copy in weights:
        copy.wait()

    @pl.loop(0, CHUNKS)
    def _(c):
        here = tokens.at[c]
        pltpu.make_async_copy(here, here, in_sem.at[c]).wait()

        @pl.loop(0, MEMBERS // TILE // ATTN_TILES)
        def _(step):
            project(step, here, gain_attn[...][None], w_qkv, swap, qkv)

        @pl.loop(0, CHUNK, unroll=True)
        def _(b):
            attend(b, qkv, bias, ones, mix)

        @pl.loop(0, MEMBERS // TILE // MLP_TILES)
        def _(step):
            finish(
                step, here, mix, swap, w_proj, gain_mlp[...][None], w_up, w_down, done.at[c]
            )
            rows = MLP_TILES * TILE

            @pl.loop(step * rows, (step + 1) * rows)
            def _(m):
                @pl.when(m != me)
                def _():
                    pltpu.make_async_remote_copy(
                        src_ref=done.at[c, m],
                        dst_ref=out_ref.at[me, pl.ds(c * CHUNK, CHUNK)],
                        send_sem=back_sem.at[0],
                        recv_sem=out_sem.at[0],
                        device_id=(m // GRID, (m % GRID) * 2 + core),
                        device_id_type=MESH,
                    ).start()

                @pl.when(m == me)
                def _():
                    pltpu.make_async_copy(
                        done.at[c, m], out_ref.at[me, pl.ds(c * CHUNK, CHUNK)], out_sem.at[0]
                    ).start()

    pltpu.make_async_copy(out_ref, out_ref, out_sem.at[0]).wait()
    others = x_ref.at[pl.ds(0, MEMBERS - 1)]
    pltpu.make_async_copy(others, others, sent_sem.at[0]).wait()
    pltpu.make_async_copy(others, others, back_sem.at[0]).wait()


def on_device(tokens_map, gain_attn, w_qkv, w_proj, rel_bias, gain_mlp, w_up, w_down):
    hbm = pl.BlockSpec(memory_space=pl.ANY)
    vmem = pl.BlockSpec(memory_space=pltpu.VMEM)
    return pl.pallas_call(
        kernel,
        name="grid_block",
        out_shape=jax.ShapeDtypeStruct(tokens_map.shape, bf16),
        in_specs=[hbm, vmem, hbm, hbm, vmem, vmem, hbm, hbm],
        out_specs=hbm,
        scratch_shapes=[
            pltpu.VMEM((CHUNKS, MEMBERS, CHUNK, D), bf16),
            pltpu.VMEM((CHUNKS, MEMBERS, CHUNK, D), bf16),
            pltpu.VMEM((D, 3 * D), bf16),
            pltpu.VMEM((D, D), bf16),
            pltpu.VMEM((D, MLP_DIM), bf16),
            pltpu.VMEM((MLP_DIM, D), bf16),
            pltpu.VMEM((3, CHUNK, MEMBERS, D), bf16),
            pltpu.VMEM((MEMBERS // TILE, CHUNK, TILE, D), bf16),
            pltpu.VMEM((3, MEMBERS, 4 * MEMBERS), f32),
            pltpu.VMEM((HEADS, GRID, 128), f32),
            pltpu.VMEM((256, 256), bf16),
            pltpu.VMEM((256, 128), bf16),
            pltpu.SemaphoreType.DMA((4,)),
            pltpu.SemaphoreType.DMA((CHUNKS,)),
            pltpu.SemaphoreType.DMA((1,)),
            pltpu.SemaphoreType.DMA((1,)),
            pltpu.SemaphoreType.DMA((1,)),
        ],
        compiler_params=pltpu.CompilerParams(
            collective_id=0, has_side_effects=True, vmem_limit_bytes=56 * 2**20
        ),
    )(tokens_map, gain_attn, w_qkv, w_proj, rel_bias, gain_mlp, w_up, w_down)


def solution(mesh):
    placed = (P("row", "col", None), P(), P(), P(), P(), P(), P(), P())
    return jax.shard_map(
        on_device, mesh=mesh, in_specs=placed, out_specs=P("row", "col", None), check_vma=False
    )
```

```python
import math

import jax
import jax.numpy as jnp
from jax import lax
from jax.experimental import pallas as pl
from jax.experimental.pallas import tpu as pltpu
from jax.sharding import PartitionSpec as P

MESH = pl.DeviceIdType.MESH
f32, bf16 = jnp.float32, jnp.bfloat16

D = 384
HEADS = 12
HEAD_DIM = 32
MLP_DIM = 1536
GRID = 8
MEMBERS = GRID * GRID
EPSILON = 1e-5
LOG2E = math.log2(math.e)

CHUNK = 16
TILE = 16
CHUNKS = 4
ATTN_TILES = 4
MLP_TILES = 4


def norm(values, gain):
    average = jnp.mean(values, -1, keepdims=True)
    centered = values - average
    variance = jnp.mean(centered * centered, -1, keepdims=True)
    return (centered * lax.rsqrt(variance + EPSILON) * gain).astype(bf16)


def fill_swap(swap):
    r = lax.broadcasted_iota(jnp.int32, (256, 256), 0)
    c = lax.broadcasted_iota(jnp.int32, (256, 256), 1)
    swap[...] = ((r // 16 == c % 16) & (r % 16 == c // 16)).astype(bf16)


def fill_ones(ones):
    r = lax.broadcasted_iota(jnp.int32, (256, 128), 0)
    c = lax.broadcasted_iota(jnp.int32, (256, 128), 1)
    ones[...] = (r // MEMBERS == c // HEAD_DIM).astype(bf16)


def fill_bias(rel, strip, bias):
    s = lax.broadcasted_iota(jnp.int32, (15, 1024), 0)
    lane = lax.broadcasted_iota(jnp.int32, (15, 1024), 1)
    g2i, q, g2j = lane // 128, (lane % 128) // 8, lane % 8
    hits = ((s == g2i - g2j + 7) & (q < 15)).astype(f32)
    rows = s == 14 - q
    for h in range(HEADS):
        spread = jnp.dot(rel[h], hits, preferred_element_type=f32, precision=lax.Precision.HIGHEST)
        line = jnp.sum(jnp.where(rows, spread, 0.0), 0, keepdims=True) * LOG2E
        for g in range(GRID):
            strip[h, g:g + 1, :] = line[:, g * 128:(g + 1) * 128]
    for h in range(HEADS):
        u = strip[h]
        for g1 in range(GRID):
            at = (GRID - 1 - g1) * GRID
            lanes = slice((h % 4) * MEMBERS, (h % 4 + 1) * MEMBERS)
            bias[h // 4, g1 * GRID:(g1 + 1) * GRID, lanes] = u[:, at:at + MEMBERS]


def turn(swap, rows):
    parts = [
        jnp.dot(swap, rows[at:at + 256], preferred_element_type=f32).astype(bf16)
        for at in range(0, rows.shape[0], 256)
    ]
    return parts[0] if len(parts) == 1 else jnp.concatenate(parts, 0)


def project(step, tokens, gain, w_qkv, swap, qkv):
    first = step * ATTN_TILES * TILE
    x = tokens[pl.ds(first, ATTN_TILES * TILE)].reshape(ATTN_TILES * 256, D).astype(f32)
    turned = turn(swap[...], norm(x, gain))
    packed = jnp.dot(turned, w_qkv[...], preferred_element_type=f32).astype(bf16)
    for part in range(3):
        for t in range(ATTN_TILES):
            block = packed[t * 256:(t + 1) * 256, part * D:(part + 1) * D]
            qkv[part, :, pl.ds(first + t * TILE, TILE), :] = block.reshape(CHUNK, TILE, D)


def attend(b, qkv, bias, ones, mix):
    lane = lax.broadcasted_iota(jnp.int32, (1, 128), 1)
    low = lane < MEMBERS
    masks = [(lane // HEAD_DIM == h).astype(bf16) for h in range(4)]
    for hb in range(3):
        cols = slice(hb * 128, (hb + 1) * 128)
        q = qkv[0, b, :, cols]
        k = qkv[1, b, :, cols]
        v = qkv[2, b, :, cols]
        keys = jnp.concatenate([k * m for m in masks], 0)
        values = jnp.concatenate([v * m for m in masks], 0)
        scores = lax.dot_general(q, keys, (((1,), (1,)), ((), ())), preferred_element_type=f32)
        scores = scores * (HEAD_DIM ** -0.5 * LOG2E) + bias[hb]
        weights = []
        for pair in range(2):
            s = scores[:, pair * 128:(pair + 1) * 128]
            peak0 = jnp.max(jnp.where(low, s, -jnp.inf), -1, keepdims=True)
            peak1 = jnp.max(jnp.where(low, -jnp.inf, s), -1, keepdims=True)
            weights.append(jnp.exp2(s - jnp.where(low, peak0, peak1)).astype(bf16))
        sums = jnp.dot(
            jnp.concatenate(weights, 1),
            jnp.concatenate([values, ones[...]], 1),
            preferred_element_type=f32,
        )
        mixture = (sums[:, :128] / sums[:, 128:]).astype(bf16)
        mix[:, pl.ds(b, 1), :, cols] = mixture.reshape(MEMBERS // TILE, 1, TILE, 128)


def finish(step, tokens, mix, swap, w_proj, gain, w_up, w_down, done):
    rows = MLP_TILES * 256
    first = step * MLP_TILES * TILE
    x = tokens[pl.ds(first, MLP_TILES * TILE)].reshape(rows, D).astype(f32)
    mixture = turn(swap[...], mix[pl.ds(step * MLP_TILES, MLP_TILES)].reshape(rows, D))
    attended = (x + jnp.dot(mixture, w_proj[...], preferred_element_type=f32)).astype(bf16)
    normed = norm(attended.astype(f32), gain)
    hidden = []
    for c in range(0, MLP_DIM, 512):
        u = jnp.dot(normed, w_up[:, c:c + 512], preferred_element_type=f32)
        hidden.append((u * (0.5 * lax.erf(u * (2 ** -0.5)) + 0.5)).astype(bf16))
    total = attended.astype(f32) + jnp.dot(
        jnp.concatenate(hidden, 1), w_down[...], preferred_element_type=f32
    )
    done[pl.ds(first, MLP_TILES * TILE)] = total.astype(bf16).reshape(MLP_TILES * TILE, CHUNK, D)


def kernel(
    x_ref, gain_attn, wq_ref, wp_ref, rel, gain_mlp, wu_ref, wd_ref,
    out_ref,
    tokens, done, w_qkv, w_proj, w_up, w_down, qkv, mix, bias, strip, swap, ones,
    weight_sem, in_sem, sent_sem, back_sem, out_sem,
):
    g1 = lax.axis_index("row")
    col = lax.axis_index("col")
    g2, core = col // 2, col % 2
    me = g1 * GRID + g2

    def partner(t):
        p1, p2 = lax.rem(g1 + t // GRID, GRID), lax.rem(g2 + lax.rem(t, GRID), GRID)
        return p1 * GRID + p2, (p1, p2 * 2 + core)

    barrier = pltpu.get_barrier_semaphore()

    @pl.loop(1, MEMBERS)
    def _(t):
        pl.semaphore_signal(barrier, inc=1, device_id=partner(t)[1], device_id_type=MESH)

    weights = [
        pltpu.make_async_copy(src, dst, weight_sem.at[i])
        for i, (src, dst) in enumerate(
            ((wq_ref, w_qkv), (wp_ref, w_proj), (wu_ref, w_up), (wd_ref, w_down))
        )
    ]
    for c in range(CHUNKS):
        pltpu.make_async_copy(
            x_ref.at[me, pl.ds(c * CHUNK, CHUNK)], tokens.at[c, me], in_sem.at[c]
        ).start()
    for copy in weights:
        copy.start()
    pl.semaphore_wait(barrier, MEMBERS - 1)

    for c in range(CHUNKS):

        @pl.loop(1, MEMBERS)
        def _(t):
            peer, device = partner(t)
            pltpu.make_async_remote_copy(
                src_ref=x_ref.at[peer, pl.ds(c * CHUNK, CHUNK)],
                dst_ref=tokens.at[c, me],
                send_sem=sent_sem.at[0],
                recv_sem=in_sem.at[c],
                device_id=device,
                device_id_type=MESH,
            ).start()

    fill_swap(swap)
    fill_ones(ones)
    fill_bias(rel, strip, bias)
    for copy in weights:
        copy.wait()

    @pl.loop(0, CHUNKS)
    def _(c):
        here = tokens.at[c]
        pltpu.make_async_copy(here, here, in_sem.at[c]).wait()

        @pl.loop(0, MEMBERS // TILE // ATTN_TILES)
        def _(step):
            project(step, here, gain_attn[...][None], w_qkv, swap, qkv)

        @pl.loop(0, CHUNK, unroll=True)
        def _(b):
            attend(b, qkv, bias, ones, mix)

        @pl.loop(0, MEMBERS // TILE // MLP_TILES)
        def _(step):
            finish(
                step, here, mix, swap, w_proj, gain_mlp[...][None], w_up, w_down, done.at[c]
            )

        @pl.loop(1, MEMBERS)
        def _(t):
            m, device = partner(t)
            pltpu.make_async_remote_copy(
                src_ref=done.at[c, m],
                dst_ref=out_ref.at[me, pl.ds(c * CHUNK, CHUNK)],
                send_sem=back_sem.at[0],
                recv_sem=out_sem.at[0],
                device_id=device,
                device_id_type=MESH,
            ).start()

        pltpu.make_async_copy(
            done.at[c, me], out_ref.at[me, pl.ds(c * CHUNK, CHUNK)], out_sem.at[0]
        ).start()

    pltpu.make_async_copy(out_ref, out_ref, out_sem.at[0]).wait()
    others = x_ref.at[pl.ds(0, MEMBERS - 1)]
    pltpu.make_async_copy(others, others, sent_sem.at[0]).wait()
    pltpu.make_async_copy(others, others, back_sem.at[0]).wait()


def on_device(tokens_map, gain_attn, w_qkv, w_proj, rel_bias, gain_mlp, w_up, w_down):
    hbm = pl.BlockSpec(memory_space=pl.ANY)
    vmem = pl.BlockSpec(memory_space=pltpu.VMEM)
    return pl.pallas_call(
        kernel,
        name="grid_block",
        out_shape=jax.ShapeDtypeStruct(tokens_map.shape, bf16),
        in_specs=[hbm, vmem, hbm, hbm, vmem, vmem, hbm, hbm],
        out_specs=hbm,
        scratch_shapes=[
            pltpu.VMEM((CHUNKS, MEMBERS, CHUNK, D), bf16),
            pltpu.VMEM((CHUNKS, MEMBERS, CHUNK, D), bf16),
            pltpu.VMEM((D, 3 * D), bf16),
            pltpu.VMEM((D, D), bf16),
            pltpu.VMEM((D, MLP_DIM), bf16),
            pltpu.VMEM((MLP_DIM, D), bf16),
            pltpu.VMEM((3, CHUNK, MEMBERS, D), bf16),
            pltpu.VMEM((MEMBERS // TILE, CHUNK, TILE, D), bf16),
            pltpu.VMEM((3, MEMBERS, 4 * MEMBERS), f32),
            pltpu.VMEM((HEADS, GRID, 128), f32),
            pltpu.VMEM((256, 256), bf16),
            pltpu.VMEM((256, 128), bf16),
            pltpu.SemaphoreType.DMA((4,)),
            pltpu.SemaphoreType.DMA((CHUNKS,)),
            pltpu.SemaphoreType.DMA((1,)),
            pltpu.SemaphoreType.DMA((1,)),
            pltpu.SemaphoreType.DMA((1,)),
        ],
        compiler_params=pltpu.CompilerParams(
            collective_id=0, has_side_effects=True, vmem_limit_bytes=56 * 2**20
        ),
    )(tokens_map, gain_attn, w_qkv, w_proj, rel_bias, gain_mlp, w_up, w_down)


def solution(mesh):
    placed = (P("row", "col", None), P(), P(), P(), P(), P(), P(), P())
    return jax.shard_map(
        on_device, mesh=mesh, in_specs=placed, out_specs=P("row", "col", None), check_vma=False
    )
```

```python
import math

import jax
import jax.numpy as jnp
from jax import lax
from jax.experimental import pallas as pl
from jax.experimental.pallas import tpu as pltpu
from jax.sharding import PartitionSpec as P

MESH = pl.DeviceIdType.MESH
f32, bf16 = jnp.float32, jnp.bfloat16

D = 384
HEADS = 12
HEAD_DIM = 32
MLP_DIM = 1536
GRID = 8
MEMBERS = GRID * GRID
EPSILON = 1e-5
LOG2E = math.log2(math.e)

CHUNK = 16
TILE = 16
CHUNKS = 4
TILES = MEMBERS // TILE


def displacements():
    def hops(d):
        return sum(min(v, 4 - v) for v in d)

    order = []
    for d in sorted(((x, y, z) for x in range(4) for y in range(4) for z in range(4)), key=hops):
        group = []
        for base in (d, tuple((4 - v) % 4 for v in d)):
            group += [base[k:] + base[:k] for k in range(3)]
        if d != (0, 0, 0) and d not in sum(order, []):
            order.append(list(dict.fromkeys(group)))
    return sum(reversed(order), [])


ORDER = displacements()


def norm(values, gain):
    average = jnp.mean(values, -1, keepdims=True)
    centered = values - average
    variance = jnp.mean(centered * centered, -1, keepdims=True)
    return (centered * lax.rsqrt(variance + EPSILON) * gain).astype(bf16)


def fill_swap(swap):
    r = lax.broadcasted_iota(jnp.int32, (256, 256), 0)
    c = lax.broadcasted_iota(jnp.int32, (256, 256), 1)
    swap[...] = ((r // 16 == c % 16) & (r % 16 == c // 16)).astype(bf16)


def fill_ones(ones):
    r = lax.broadcasted_iota(jnp.int32, (256, 128), 0)
    c = lax.broadcasted_iota(jnp.int32, (256, 128), 1)
    ones[...] = (r // MEMBERS == c // HEAD_DIM).astype(bf16)


def fill_bias(rel, strip, bias):
    s = lax.broadcasted_iota(jnp.int32, (15, 1024), 0)
    lane = lax.broadcasted_iota(jnp.int32, (15, 1024), 1)
    g2i, q, g2j = lane // 128, (lane % 128) // 8, lane % 8
    hits = ((s == g2i - g2j + 7) & (q < 15)).astype(f32)
    rows = s == 14 - q
    for h in range(HEADS):
        spread = jnp.dot(rel[h], hits, preferred_element_type=f32, precision=lax.Precision.HIGHEST)
        line = jnp.sum(jnp.where(rows, spread, 0.0), 0, keepdims=True) * LOG2E
        for g in range(GRID):
            strip[h, g:g + 1, :] = line[:, g * 128:(g + 1) * 128]
    for h in range(HEADS):
        u = strip[h]
        for g1 in range(GRID):
            at = (GRID - 1 - g1) * GRID
            lanes = slice((h % 4) * MEMBERS, (h % 4 + 1) * MEMBERS)
            bias[h // 4, g1 * GRID:(g1 + 1) * GRID, lanes] = u[:, at:at + MEMBERS]


def turn(swap, rows):
    parts = [
        jnp.dot(swap, rows[at:at + 256], preferred_element_type=f32).astype(bf16)
        for at in range(0, rows.shape[0], 256)
    ]
    return parts[0] if len(parts) == 1 else jnp.concatenate(parts, 0)


def project(first, tiles, tokens, gain, w_qkv, swap, qkv):
    x = tokens[pl.ds(first, tiles * TILE)].reshape(tiles * 256, D).astype(f32)
    turned = turn(swap[...], norm(x, gain))
    packed = jnp.dot(turned, w_qkv[...], preferred_element_type=f32).astype(bf16)
    for part in range(3):
        for t in range(tiles):
            block = packed[t * 256:(t + 1) * 256, part * D:(part + 1) * D]
            qkv[part, :, pl.ds(first + t * TILE, TILE), :] = block.reshape(CHUNK, TILE, D)


def attend(b, qkv, bias, ones, mix):
    lane = lax.broadcasted_iota(jnp.int32, (1, 128), 1)
    low = lane < MEMBERS
    masks = [(lane // HEAD_DIM == h).astype(bf16) for h in range(4)]
    for hb in range(3):
        cols = slice(hb * 128, (hb + 1) * 128)
        q = qkv[0, b, :, cols]
        k = qkv[1, b, :, cols]
        v = qkv[2, b, :, cols]
        keys = jnp.concatenate([k * m for m in masks], 0)
        values = jnp.concatenate([v * m for m in masks], 0)
        scores = lax.dot_general(q, keys, (((1,), (1,)), ((), ())), preferred_element_type=f32)
        scores = scores * (HEAD_DIM ** -0.5 * LOG2E) + bias[hb]
        weights = []
        for pair in range(2):
            s = scores[:, pair * 128:(pair + 1) * 128]
            peak0 = jnp.max(jnp.where(low, s, -jnp.inf), -1, keepdims=True)
            peak1 = jnp.max(jnp.where(low, -jnp.inf, s), -1, keepdims=True)
            weights.append(jnp.exp2(s - jnp.where(low, peak0, peak1)).astype(bf16))
        sums = jnp.dot(
            jnp.concatenate(weights, 1),
            jnp.concatenate([values, ones[...]], 1),
            preferred_element_type=f32,
        )
        mixture = (sums[:, :128] / sums[:, 128:]).astype(bf16)
        mix[:, pl.ds(b, 1), :, cols] = mixture.reshape(MEMBERS // TILE, 1, TILE, 128)


def finish(first, tiles, tokens, mix, swap, w_proj, gain, w_up, w_down, done):
    rows = tiles * 256
    x = tokens[pl.ds(first * TILE, tiles * TILE)].reshape(rows, D).astype(f32)
    mixture = turn(swap[...], mix[pl.ds(first, tiles)].reshape(rows, D))
    attended = (x + jnp.dot(mixture, w_proj[...], preferred_element_type=f32)).astype(bf16)
    normed = norm(attended.astype(f32), gain)
    hidden = []
    for c in range(0, MLP_DIM, 512):
        u = jnp.dot(normed, w_up[:, c:c + 512], preferred_element_type=f32)
        hidden.append((u * (0.5 * lax.erf(u * (2 ** -0.5)) + 0.5)).astype(bf16))
    total = attended.astype(f32) + jnp.dot(
        jnp.concatenate(hidden, 1), w_down[...], preferred_element_type=f32
    )
    done[pl.ds(first * TILE, tiles * TILE)] = total.astype(bf16).reshape(tiles * TILE, CHUNK, D)


def kernel(
    x_ref, ga_ref, wq_ref, wp_ref, rb_ref, gm_ref, wu_ref, wd_ref,
    out_ref,
    tokens, done, gain_attn, gain_mlp, rel, w_qkv, w_proj, w_up, w_down, qkv, mix, bias, strip, swap, ones,
    weight_sem, in_sem, sent_sem, back_sem, out_sem,
):
    g1 = lax.axis_index("row")
    col = lax.axis_index("col")
    g2, core = lax.div(col, 2), lax.rem(col, 2)
    me = g1 * GRID + g2
    z_lo, x = lax.div(g1, 4), lax.rem(g1, 4)
    y, z = lax.div(g2, 2), lax.rem(g2, 2) * 2 + z_lo
    xs, ys, zs = ([lax.rem(v + k, 4) for k in range(4)] for v in (x, y, z))
    z_highs = [lax.div(v, 2) for v in zs]
    z_lows = [lax.rem(v, 2) for v in zs]

    def partner(d):
        p1 = z_lows[d[2]] * 4 + xs[d[0]]
        p2 = ys[d[1]] * 2 + z_highs[d[2]]
        return p1 * GRID + p2, (p1, p2 * 2 + core)

    barrier = pltpu.get_barrier_semaphore()
    for d in ORDER:
        pl.semaphore_signal(barrier, inc=1, device_id=partner(d)[1], device_id_type=MESH)

    local = [
        pltpu.make_async_copy(src, dst, weight_sem.at[i])
        for i, (src, dst) in enumerate((
            (rb_ref, rel), (ga_ref, gain_attn), (wq_ref, w_qkv), (wp_ref, w_proj),
            (gm_ref, gain_mlp), (wu_ref, w_up), (wd_ref, w_down),
        ))
    ]
    for copy in local:
        copy.start()
    for c in range(CHUNKS):
        pltpu.make_async_copy(
            x_ref.at[me, pl.ds(c * CHUNK, CHUNK)], tokens.at[c, me], in_sem.at[c]
        ).start()
    pl.semaphore_wait(barrier, MEMBERS - 1)

    def send(c):
        for d in ORDER:
            peer, device = partner(d)
            pltpu.make_async_remote_copy(
                src_ref=x_ref.at[peer, pl.ds(c * CHUNK, CHUNK)],
                dst_ref=tokens.at[c, me],
                send_sem=sent_sem.at[0],
                recv_sem=in_sem.at[c],
                device_id=device,
                device_id_type=MESH,
            ).start()

    def send_back(c, order):
        for d in order:
            peer, device = partner(d)
            pltpu.make_async_remote_copy(
                src_ref=done.at[c, peer],
                dst_ref=out_ref.at[me, pl.ds(c * CHUNK, CHUNK)],
                send_sem=back_sem.at[0],
                recv_sem=out_sem.at[0],
                device_id=device,
                device_id_type=MESH,
            ).start()

    def keep(c):
        pltpu.make_async_copy(
            done.at[c, me], out_ref.at[me, pl.ds(c * CHUNK, CHUNK)], out_sem.at[0]
        ).start()

    send(0)
    send(1)
    fill_swap(swap)
    fill_ones(ones)
    local[0].wait()
    fill_bias(rel, strip, bias)
    for copy in local[1:]:
        copy.wait()

    def attention(c):
        here = tokens.at[c]
        pltpu.make_async_copy(here, here, in_sem.at[c]).wait()
        project(0, TILES, here, gain_attn[...][None], w_qkv, swap, qkv)
        if not isinstance(c, int):

            @pl.when(c < CHUNKS - 2)
            def _():
                send(c + 2)

        @pl.loop(0, CHUNK, unroll=True)
        def _(b):
            attend(b, qkv, bias, ones, mix)

    def rest(c, first, tiles):
        finish(
            first, tiles, tokens.at[c], mix, swap, w_proj, gain_mlp[...][None], w_up, w_down, done.at[c]
        )

    @pl.loop(0, CHUNKS - 1)
    def _(c):
        attention(c)
        rest(c, 0, TILES)
        send_back(c, ORDER)
        keep(c)

    last = CHUNKS - 1
    attention(last)
    rest(last, (1 - z_lo) * 2, 2)
    send_back(last, [d for d in ORDER if d[2] % 2 == 1])
    rest(last, z_lo * 2, 2)
    send_back(last, [d for d in ORDER if d[2] % 2 == 0])
    keep(last)

    pltpu.make_async_copy(out_ref, out_ref, out_sem.at[0]).wait()
    others = x_ref.at[pl.ds(0, MEMBERS - 1)]
    pltpu.make_async_copy(others, others, sent_sem.at[0]).wait()
    pltpu.make_async_copy(others, others, back_sem.at[0]).wait()


def move(src, dst, sems):
    parts = sems.shape[0]
    step = src.shape[0] // parts
    copies = [
        pltpu.make_async_copy(src.at[pl.ds(i * step, step)], dst.at[pl.ds(i * step, step)], sems.at[i])
        for i in range(parts)
    ]
    for copy in copies:
        copy.start()
    for copy in copies:
        copy.wait()


def on_device(tokens_map, gain_attn, w_qkv, w_proj, rel_bias, gain_mlp, w_up, w_down):
    hbm = pl.BlockSpec(memory_space=pltpu.HBM)
    arrived = pl.pallas_call(
        kernel,
        name="grid_block",
        out_shape=pltpu.VMEM(tokens_map.shape, bf16),
        in_specs=[hbm] * 8,
        out_specs=pl.BlockSpec(memory_space=pl.ANY),
        scratch_shapes=[
            pltpu.VMEM((CHUNKS, MEMBERS, CHUNK, D), bf16),
            pltpu.VMEM((CHUNKS, MEMBERS, CHUNK, D), bf16),
            pltpu.VMEM((D,), f32),
            pltpu.VMEM((D,), f32),
            pltpu.VMEM((HEADS, 15, 15), f32),
            pltpu.VMEM((D, 3 * D), bf16),
            pltpu.VMEM((D, D), bf16),
            pltpu.VMEM((D, MLP_DIM), bf16),
            pltpu.VMEM((MLP_DIM, D), bf16),
            pltpu.VMEM((3, CHUNK, MEMBERS, D), bf16),
            pltpu.VMEM((MEMBERS // TILE, CHUNK, TILE, D), bf16),
            pltpu.VMEM((3, MEMBERS, 4 * MEMBERS), f32),
            pltpu.VMEM((HEADS, GRID, 128), f32),
            pltpu.VMEM((256, 256), bf16),
            pltpu.VMEM((256, 128), bf16),
            pltpu.SemaphoreType.DMA((7,)),
            pltpu.SemaphoreType.DMA((CHUNKS,)),
            pltpu.SemaphoreType.DMA((1,)),
            pltpu.SemaphoreType.DMA((1,)),
            pltpu.SemaphoreType.DMA((1,)),
        ],
        compiler_params=pltpu.CompilerParams(
            collective_id=0, has_side_effects=True, vmem_limit_bytes=44 * 2**20
        ),
    )(*(pltpu.with_memory_space_constraint(a, pltpu.HBM) for a in (tokens_map, gain_attn, w_qkv, w_proj, rel_bias, gain_mlp, w_up, w_down)))
    return pl.pallas_call(
        move,
        name="move_out",
        out_shape=jax.ShapeDtypeStruct(tokens_map.shape, bf16),
        in_specs=[pl.BlockSpec(memory_space=pl.ANY)],
        out_specs=hbm,
        scratch_shapes=[pltpu.SemaphoreType.DMA((8,))],
        compiler_params=pltpu.CompilerParams(vmem_limit_bytes=16 * 2**20),
    )(arrived)


def solution(mesh):
    placed = (P("row", "col", None), P(), P(), P(), P(), P(), P(), P())
    return jax.shard_map(
        on_device, mesh=mesh, in_specs=placed, out_specs=P("row", "col", None), check_vma=False
    )
```

```python
import math

import jax
import jax.numpy as jnp
from jax import lax
from jax.experimental import pallas as pl
from jax.experimental.pallas import tpu as pltpu
from jax.sharding import PartitionSpec as P

MESH = pl.DeviceIdType.MESH
f32, bf16 = jnp.float32, jnp.bfloat16

D = 384
HEADS = 12
HEAD_DIM = 32
MLP_DIM = 1536
GRID = 8
MEMBERS = GRID * GRID
EPSILON = 1e-5
LOG2E = math.log2(math.e)

CHUNK = 16
TILE = 16
CHUNKS = 4
TILES = MEMBERS // TILE


def displacements():
    def hops(d):
        return sum(min(v, 4 - v) for v in d)

    order = []
    for d in sorted(((x, y, z) for x in range(4) for y in range(4) for z in range(4)), key=hops):
        group = []
        for base in (d, tuple((4 - v) % 4 for v in d)):
            group += [base[k:] + base[:k] for k in range(3)]
        if d != (0, 0, 0) and d not in sum(order, []):
            order.append(list(dict.fromkeys(group)))
    return sum(reversed(order), [])


ORDER = displacements()
LINES, PLANES, SPACE = ([d for d in ORDER if d.count(0) == 3 - n] for n in (1, 2, 3))


def norm(values, gain):
    average = jnp.mean(values, -1, keepdims=True)
    centered = values - average
    variance = jnp.mean(centered * centered, -1, keepdims=True)
    return (centered * lax.rsqrt(variance + EPSILON) * gain).astype(bf16)


def fill_swap(swap):
    r = lax.broadcasted_iota(jnp.int32, (256, 256), 0)
    c = lax.broadcasted_iota(jnp.int32, (256, 256), 1)
    swap[...] = ((r // 16 == c % 16) & (r % 16 == c // 16)).astype(bf16)


def fill_ones(ones):
    r = lax.broadcasted_iota(jnp.int32, (256, 128), 0)
    c = lax.broadcasted_iota(jnp.int32, (256, 128), 1)
    ones[...] = (r // MEMBERS == c // HEAD_DIM).astype(bf16)


def fill_bias(rel, strip, bias):
    s = lax.broadcasted_iota(jnp.int32, (15, 1024), 0)
    lane = lax.broadcasted_iota(jnp.int32, (15, 1024), 1)
    g2i, q, g2j = lane // 128, (lane % 128) // 8, lane % 8
    hits = ((s == g2i - g2j + 7) & (q < 15)).astype(f32)
    rows = s == 14 - q
    for h in range(HEADS):
        spread = jnp.dot(rel[h], hits, preferred_element_type=f32, precision=lax.Precision.HIGHEST)
        line = jnp.sum(jnp.where(rows, spread, 0.0), 0, keepdims=True) * LOG2E
        for g in range(GRID):
            strip[h, g:g + 1, :] = line[:, g * 128:(g + 1) * 128]
    for h in range(HEADS):
        u = strip[h]
        for g1 in range(GRID):
            at = (GRID - 1 - g1) * GRID
            lanes = slice((h % 4) * MEMBERS, (h % 4 + 1) * MEMBERS)
            bias[h // 4, g1 * GRID:(g1 + 1) * GRID, lanes] = u[:, at:at + MEMBERS]


def turn(swap, rows):
    parts = [
        jnp.dot(swap, rows[at:at + 256], preferred_element_type=f32).astype(bf16)
        for at in range(0, rows.shape[0], 256)
    ]
    return parts[0] if len(parts) == 1 else jnp.concatenate(parts, 0)


def project(first, tiles, tokens, gain, w_qkv, swap, qkv):
    x = tokens[pl.ds(first, tiles * TILE)].reshape(tiles * 256, D).astype(f32)
    turned = turn(swap[...], norm(x, gain))
    packed = jnp.dot(turned, w_qkv[...], preferred_element_type=f32).astype(bf16)
    for part in range(3):
        for t in range(tiles):
            block = packed[t * 256:(t + 1) * 256, part * D:(part + 1) * D]
            qkv[part, :, pl.ds(first + t * TILE, TILE), :] = block.reshape(CHUNK, TILE, D)


def attend(b, qkv, bias, ones, mix):
    lane = lax.broadcasted_iota(jnp.int32, (1, 128), 1)
    low = lane < MEMBERS
    masks = [(lane // HEAD_DIM == h).astype(bf16) for h in range(4)]
    for hb in range(3):
        cols = slice(hb * 128, (hb + 1) * 128)
        q = qkv[0, b, :, cols]
        k = qkv[1, b, :, cols]
        v = qkv[2, b, :, cols]
        keys = jnp.concatenate([k * m for m in masks], 0)
        values = jnp.concatenate([v * m for m in masks], 0)
        scores = lax.dot_general(q, keys, (((1,), (1,)), ((), ())), preferred_element_type=f32)
        scores = scores * (HEAD_DIM ** -0.5 * LOG2E) + bias[hb]
        weights = []
        for pair in range(2):
            s = scores[:, pair * 128:(pair + 1) * 128]
            peak0 = jnp.max(jnp.where(low, s, -jnp.inf), -1, keepdims=True)
            peak1 = jnp.max(jnp.where(low, -jnp.inf, s), -1, keepdims=True)
            weights.append(jnp.exp2(s - jnp.where(low, peak0, peak1)).astype(bf16))
        sums = jnp.dot(
            jnp.concatenate(weights, 1),
            jnp.concatenate([values, ones[...]], 1),
            preferred_element_type=f32,
        )
        mixture = (sums[:, :128] / sums[:, 128:]).astype(bf16)
        mix[:, pl.ds(b, 1), :, cols] = mixture.reshape(MEMBERS // TILE, 1, TILE, 128)


def finish(first, tiles, tokens, mix, swap, w_proj, gain, w_up, w_down, done):
    rows = tiles * 256
    x = tokens[pl.ds(first * TILE, tiles * TILE)].reshape(rows, D).astype(f32)
    mixture = turn(swap[...], mix[pl.ds(first, tiles)].reshape(rows, D))
    attended = (x + jnp.dot(mixture, w_proj[...], preferred_element_type=f32)).astype(bf16)
    normed = norm(attended.astype(f32), gain)
    hidden = []
    for c in range(0, MLP_DIM, 512):
        u = jnp.dot(normed, w_up[:, c:c + 512], preferred_element_type=f32)
        hidden.append((u * (0.5 * lax.erf(u * (2 ** -0.5)) + 0.5)).astype(bf16))
    total = attended.astype(f32) + jnp.dot(
        jnp.concatenate(hidden, 1), w_down[...], preferred_element_type=f32
    )
    done[pl.ds(first * TILE, tiles * TILE)] = total.astype(bf16).reshape(tiles * TILE, CHUNK, D)


def kernel(
    x_ref, ga_ref, wq_ref, wp_ref, rb_ref, gm_ref, wu_ref, wd_ref,
    out_ref,
    tokens, done, gain_attn, gain_mlp, rel, w_qkv, w_proj, w_up, w_down, qkv, mix, bias, strip, swap, ones,
    heard, weight_sem, in_sem, sent_sem, back_sem, out_sem,
):
    g1 = lax.axis_index("row")
    col = lax.axis_index("col")
    g2, core = lax.div(col, 2), lax.rem(col, 2)
    me = g1 * GRID + g2
    z_lo, x = lax.div(g1, 4), lax.rem(g1, 4)
    y, z = lax.div(g2, 2), lax.rem(g2, 2) * 2 + z_lo
    xs, ys, zs = ([lax.rem(v + k, 4) for k in range(4)] for v in (x, y, z))
    z_highs = [lax.div(v, 2) for v in zs]
    z_lows = [lax.rem(v, 2) for v in zs]

    def partner(d):
        p1 = z_lows[d[2]] * 4 + xs[d[0]]
        p2 = ys[d[1]] * 2 + z_highs[d[2]]
        return p1 * GRID + p2, (p1, p2 * 2 + core)

    barrier = pltpu.get_barrier_semaphore()
    for d in LINES:
        pl.semaphore_signal(barrier, inc=1, device_id=partner(d)[1], device_id_type=MESH)

    local = [
        pltpu.make_async_copy(src, dst, weight_sem.at[i])
        for i, (src, dst) in enumerate((
            (rb_ref, rel), (ga_ref, gain_attn), (wq_ref, w_qkv), (wp_ref, w_proj),
            (gm_ref, gain_mlp), (wu_ref, w_up), (wd_ref, w_down),
        ))
    ]
    for copy in local:
        copy.start()
    for c in range(CHUNKS):
        pltpu.make_async_copy(
            x_ref.at[me, pl.ds(c * CHUNK, CHUNK)], tokens.at[c, me], in_sem.at[c]
        ).start()

    def send(c, order):
        for d in order:
            peer, device = partner(d)
            pltpu.make_async_remote_copy(
                src_ref=x_ref.at[peer, pl.ds(c * CHUNK, CHUNK)],
                dst_ref=tokens.at[c, me],
                send_sem=sent_sem.at[0],
                recv_sem=in_sem.at[c],
                device_id=device,
                device_id_type=MESH,
            ).start()

    def send_back(c, order):
        for d in order:
            peer, device = partner(d)
            pltpu.make_async_remote_copy(
                src_ref=done.at[c, peer],
                dst_ref=out_ref.at[me, pl.ds(c * CHUNK, CHUNK)],
                send_sem=back_sem.at[0],
                recv_sem=out_sem.at[0],
                device_id=device,
                device_id_type=MESH,
            ).start()

    def keep(c):
        pltpu.make_async_copy(
            done.at[c, me], out_ref.at[me, pl.ds(c * CHUNK, CHUNK)], out_sem.at[0]
        ).start()

    def tell(round_):
        for d in LINES:
            pl.semaphore_signal(
                heard.at[round_], inc=1, device_id=partner(d)[1], device_id_type=MESH
            )

    pl.semaphore_wait(barrier, len(LINES))
    tell(0)
    for c in range(CHUNKS):
        send(c, LINES)
    pl.semaphore_wait(heard.at[0], len(LINES))
    tell(1)
    send(0, PLANES)
    pl.semaphore_wait(heard.at[1], len(LINES))
    send(0, SPACE)
    send(1, SPACE + PLANES)
    fill_swap(swap)
    fill_ones(ones)
    local[0].wait()
    fill_bias(rel, strip, bias)
    for copy in local[1:]:
        copy.wait()

    def attention(c):
        here = tokens.at[c]
        pltpu.make_async_copy(here, here, in_sem.at[c]).wait()
        project(0, TILES, here, gain_attn[...][None], w_qkv, swap, qkv)
        if not isinstance(c, int):

            @pl.when(c < CHUNKS - 2)
            def _():
                send(c + 2, SPACE + PLANES)

        @pl.loop(0, CHUNK, unroll=True)
        def _(b):
            attend(b, qkv, bias, ones, mix)

    def rest(c, first, tiles):
        finish(
            first, tiles, tokens.at[c], mix, swap, w_proj, gain_mlp[...][None], w_up, w_down, done.at[c]
        )

    @pl.loop(0, CHUNKS - 1)
    def _(c):
        attention(c)
        rest(c, 0, TILES)
        send_back(c, ORDER)
        keep(c)

    last = CHUNKS - 1
    attention(last)
    rest(last, (1 - z_lo) * 2, 2)
    send_back(last, [d for d in ORDER if d[2] % 2 == 1])
    rest(last, z_lo * 2, 2)
    send_back(last, [d for d in ORDER if d[2] % 2 == 0])
    keep(last)

    pltpu.make_async_copy(out_ref, out_ref, out_sem.at[0]).wait()
    others = x_ref.at[pl.ds(0, MEMBERS - 1)]
    pltpu.make_async_copy(others, others, sent_sem.at[0]).wait()
    pltpu.make_async_copy(others, others, back_sem.at[0]).wait()


def move(src, dst, sems):
    parts = sems.shape[0]
    step = src.shape[0] // parts
    copies = [
        pltpu.make_async_copy(src.at[pl.ds(i * step, step)], dst.at[pl.ds(i * step, step)], sems.at[i])
        for i in range(parts)
    ]
    for copy in copies:
        copy.start()
    for copy in copies:
        copy.wait()


def on_device(tokens_map, gain_attn, w_qkv, w_proj, rel_bias, gain_mlp, w_up, w_down):
    hbm = pl.BlockSpec(memory_space=pltpu.HBM)
    arrived = pl.pallas_call(
        kernel,
        name="grid_block",
        out_shape=pltpu.VMEM(tokens_map.shape, bf16),
        in_specs=[hbm] * 8,
        out_specs=pl.BlockSpec(memory_space=pl.ANY),
        scratch_shapes=[
            pltpu.VMEM((CHUNKS, MEMBERS, CHUNK, D), bf16),
            pltpu.VMEM((CHUNKS, MEMBERS, CHUNK, D), bf16),
            pltpu.VMEM((D,), f32),
            pltpu.VMEM((D,), f32),
            pltpu.VMEM((HEADS, 15, 15), f32),
            pltpu.VMEM((D, 3 * D), bf16),
            pltpu.VMEM((D, D), bf16),
            pltpu.VMEM((D, MLP_DIM), bf16),
            pltpu.VMEM((MLP_DIM, D), bf16),
            pltpu.VMEM((3, CHUNK, MEMBERS, D), bf16),
            pltpu.VMEM((MEMBERS // TILE, CHUNK, TILE, D), bf16),
            pltpu.VMEM((3, MEMBERS, 4 * MEMBERS), f32),
            pltpu.VMEM((HEADS, GRID, 128), f32),
            pltpu.VMEM((256, 256), bf16),
            pltpu.VMEM((256, 128), bf16),
            pltpu.SemaphoreType.REGULAR((2,)),
            pltpu.SemaphoreType.DMA((7,)),
            pltpu.SemaphoreType.DMA((CHUNKS,)),
            pltpu.SemaphoreType.DMA((1,)),
            pltpu.SemaphoreType.DMA((1,)),
            pltpu.SemaphoreType.DMA((1,)),
        ],
        compiler_params=pltpu.CompilerParams(
            collective_id=0, has_side_effects=True, vmem_limit_bytes=44 * 2**20
        ),
    )(*(pltpu.with_memory_space_constraint(a, pltpu.HBM) for a in (tokens_map, gain_attn, w_qkv, w_proj, rel_bias, gain_mlp, w_up, w_down)))
    return pl.pallas_call(
        move,
        name="move_out",
        out_shape=jax.ShapeDtypeStruct(tokens_map.shape, bf16),
        in_specs=[pl.BlockSpec(memory_space=pl.ANY)],
        out_specs=hbm,
        scratch_shapes=[pltpu.SemaphoreType.DMA((8,))],
        compiler_params=pltpu.CompilerParams(vmem_limit_bytes=16 * 2**20),
    )(arrived)


def solution(mesh):
    placed = (P("row", "col", None), P(), P(), P(), P(), P(), P(), P())
    return jax.shard_map(
        on_device, mesh=mesh, in_specs=placed, out_specs=P("row", "col", None), check_vma=False
    )
```

```python
import math

import jax
import jax.numpy as jnp
from jax import lax
from jax.experimental import pallas as pl
from jax.experimental.pallas import tpu as pltpu
from jax.sharding import PartitionSpec as P

MESH = pl.DeviceIdType.MESH
f32, bf16 = jnp.float32, jnp.bfloat16

D = 384
HEADS = 12
HEAD_DIM = 32
MLP_DIM = 1536
GRID = 8
MEMBERS = GRID * GRID
EPSILON = 1e-5
LOG2E = math.log2(math.e)

CHUNK = 16
TILE = 16
CHUNKS = 4
TILES = MEMBERS // TILE


def displacements():
    def hops(d):
        return sum(min(v, 4 - v) for v in d)

    order = []
    for d in sorted(((x, y, z) for x in range(4) for y in range(4) for z in range(4)), key=hops):
        group = []
        for base in (d, tuple((4 - v) % 4 for v in d)):
            group += [base[k:] + base[:k] for k in range(3)]
        if d != (0, 0, 0) and d not in sum(order, []):
            order.append(list(dict.fromkeys(group)))
    return sum(reversed(order), [])


ORDER = displacements()
LINES, PLANES, SPACE = ([d for d in ORDER if d.count(0) == 3 - n] for n in (1, 2, 3))


def norm(values, gain):
    average = jnp.mean(values, -1, keepdims=True)
    centered = values - average
    variance = jnp.mean(centered * centered, -1, keepdims=True)
    return (centered * lax.rsqrt(variance + EPSILON) * gain).astype(bf16)


def fill_swap(swap):
    r = lax.broadcasted_iota(jnp.int32, (256, 256), 0)
    c = lax.broadcasted_iota(jnp.int32, (256, 256), 1)
    swap[...] = ((r // 16 == c % 16) & (r % 16 == c // 16)).astype(bf16)


def fill_ones(ones):
    r = lax.broadcasted_iota(jnp.int32, (256, 128), 0)
    c = lax.broadcasted_iota(jnp.int32, (256, 128), 1)
    ones[...] = (r // MEMBERS == c // HEAD_DIM).astype(bf16)


def fill_bias(rel, strip, bias):
    s = lax.broadcasted_iota(jnp.int32, (15, 1024), 0)
    lane = lax.broadcasted_iota(jnp.int32, (15, 1024), 1)
    g2i, q, g2j = lane // 128, (lane % 128) // 8, lane % 8
    hits = ((s == g2i - g2j + 7) & (q < 15)).astype(f32)
    rows = s == 14 - q
    for h in range(HEADS):
        spread = jnp.dot(rel[h], hits, preferred_element_type=f32, precision=lax.Precision.HIGHEST)
        line = jnp.sum(jnp.where(rows, spread, 0.0), 0, keepdims=True) * LOG2E
        for g in range(GRID):
            strip[h, g:g + 1, :] = line[:, g * 128:(g + 1) * 128]
    for h in range(HEADS):
        u = strip[h]
        for g1 in range(GRID):
            at = (GRID - 1 - g1) * GRID
            lanes = slice((h % 4) * MEMBERS, (h % 4 + 1) * MEMBERS)
            bias[h // 4, g1 * GRID:(g1 + 1) * GRID, lanes] = u[:, at:at + MEMBERS]


def turn(swap, rows):
    parts = [
        jnp.dot(swap, rows[at:at + 256], preferred_element_type=f32).astype(bf16)
        for at in range(0, rows.shape[0], 256)
    ]
    return parts[0] if len(parts) == 1 else jnp.concatenate(parts, 0)


def project(first, tiles, tokens, gain, w_qkv, swap, qkv):
    x = tokens[pl.ds(first, tiles * TILE)].reshape(tiles * 256, D).astype(f32)
    turned = turn(swap[...], norm(x, gain))
    packed = jnp.dot(turned, w_qkv[...], preferred_element_type=f32).astype(bf16)
    for part in range(3):
        for t in range(tiles):
            block = packed[t * 256:(t + 1) * 256, part * D:(part + 1) * D]
            qkv[part, :, pl.ds(first + t * TILE, TILE), :] = block.reshape(CHUNK, TILE, D)


def attend(b, qkv, bias, ones, mix):
    lane = lax.broadcasted_iota(jnp.int32, (1, 128), 1)
    low = lane < MEMBERS
    masks = [(lane // HEAD_DIM == h).astype(bf16) for h in range(4)]
    for hb in range(3):
        cols = slice(hb * 128, (hb + 1) * 128)
        q = qkv[0, b, :, cols]
        k = qkv[1, b, :, cols]
        v = qkv[2, b, :, cols]
        keys = jnp.concatenate([k * m for m in masks], 0)
        values = jnp.concatenate([v * m for m in masks], 0)
        scores = lax.dot_general(q, keys, (((1,), (1,)), ((), ())), preferred_element_type=f32)
        scores = scores * (HEAD_DIM ** -0.5 * LOG2E) + bias[hb]
        weights = []
        for pair in range(2):
            s = scores[:, pair * 128:(pair + 1) * 128]
            peak0 = jnp.max(jnp.where(low, s, -jnp.inf), -1, keepdims=True)
            peak1 = jnp.max(jnp.where(low, -jnp.inf, s), -1, keepdims=True)
            weights.append(jnp.exp2(s - jnp.where(low, peak0, peak1)).astype(bf16))
        sums = jnp.dot(
            jnp.concatenate(weights, 1),
            jnp.concatenate([values, ones[...]], 1),
            preferred_element_type=f32,
        )
        mixture = (sums[:, :128] / sums[:, 128:]).astype(bf16)
        mix[:, pl.ds(b, 1), :, cols] = mixture.reshape(MEMBERS // TILE, 1, TILE, 128)


def finish(first, tiles, tokens, mix, swap, w_proj, gain, w_up, w_down, done):
    rows = tiles * 256
    x = tokens[pl.ds(first * TILE, tiles * TILE)].reshape(rows, D).astype(f32)
    mixture = turn(swap[...], mix[pl.ds(first, tiles)].reshape(rows, D))
    attended = (x + jnp.dot(mixture, w_proj[...], preferred_element_type=f32)).astype(bf16)
    normed = norm(attended.astype(f32), gain)
    hidden = []
    for c in range(0, MLP_DIM, 512):
        u = jnp.dot(normed, w_up[:, c:c + 512], preferred_element_type=f32)
        hidden.append((u * (0.5 * lax.erf(u * (2 ** -0.5)) + 0.5)).astype(bf16))
    total = attended.astype(f32) + jnp.dot(
        jnp.concatenate(hidden, 1), w_down[...], preferred_element_type=f32
    )
    done[pl.ds(first * TILE, tiles * TILE)] = total.astype(bf16).reshape(tiles * TILE, CHUNK, D)


def kernel(
    x_ref, ga_ref, wq_ref, wp_ref, rb_ref, gm_ref, wu_ref, wd_ref,
    out_ref,
    tokens, done, gain_attn, gain_mlp, rel, w_qkv, w_proj, w_up, w_down, qkv, mix, bias, strip, swap, ones,
    heard, weight_sem, in_sem, sent_sem, back_sem, out_sem,
):
    g1 = lax.axis_index("row")
    col = lax.axis_index("col")
    g2, core = lax.div(col, 2), lax.rem(col, 2)
    me = g1 * GRID + g2
    z_lo, x = lax.div(g1, 4), lax.rem(g1, 4)
    y, z = lax.div(g2, 2), lax.rem(g2, 2) * 2 + z_lo
    xs, ys, zs = ([lax.rem(v + k, 4) for k in range(4)] for v in (x, y, z))
    z_highs = [lax.div(v, 2) for v in zs]
    z_lows = [lax.rem(v, 2) for v in zs]

    def partner(d):
        p1 = z_lows[d[2]] * 4 + xs[d[0]]
        p2 = ys[d[1]] * 2 + z_highs[d[2]]
        return p1 * GRID + p2, (p1, p2 * 2 + core)

    barrier = pltpu.get_barrier_semaphore()
    for d in LINES:
        pl.semaphore_signal(barrier, inc=1, device_id=partner(d)[1], device_id_type=MESH)

    local = [
        pltpu.make_async_copy(src, dst, weight_sem.at[i])
        for i, (src, dst) in enumerate((
            (rb_ref, rel), (ga_ref, gain_attn), (wq_ref, w_qkv), (wp_ref, w_proj),
            (gm_ref, gain_mlp), (wu_ref, w_up), (wd_ref, w_down),
        ))
    ]
    for copy in local:
        copy.start()
    for c in range(CHUNKS):
        pltpu.make_async_copy(
            x_ref.at[me, pl.ds(c * CHUNK, CHUNK)], tokens.at[c, me], in_sem.at[c]
        ).start()

    def send(c, order):
        for d in order:
            peer, device = partner(d)
            pltpu.make_async_remote_copy(
                src_ref=x_ref.at[peer, pl.ds(c * CHUNK, CHUNK)],
                dst_ref=tokens.at[c, me],
                send_sem=sent_sem.at[0],
                recv_sem=in_sem.at[c],
                device_id=device,
                device_id_type=MESH,
            ).start()

    def send_back(c, order):
        for d in order:
            peer, device = partner(d)
            pltpu.make_async_remote_copy(
                src_ref=done.at[c, peer],
                dst_ref=out_ref.at[me, pl.ds(c * CHUNK, CHUNK)],
                send_sem=back_sem.at[0],
                recv_sem=out_sem.at[0],
                device_id=device,
                device_id_type=MESH,
            ).start()

    def keep(c):
        pltpu.make_async_copy(
            done.at[c, me], out_ref.at[me, pl.ds(c * CHUNK, CHUNK)], out_sem.at[0]
        ).start()

    def tell(round_, mates):
        for d in mates:
            pl.semaphore_signal(
                heard.at[round_], inc=1, device_id=partner(d)[1], device_id_type=MESH
            )

    along_z = [d for d in LINES if d[2]]
    across = [d for d in LINES if not d[2]]
    pl.semaphore_wait(barrier, len(LINES))
    tell(0, across)
    for c in range(CHUNKS):
        send(c, LINES)
    pl.semaphore_wait(heard.at[0], len(across))
    tell(1, along_z)
    send(0, PLANES)
    pl.semaphore_wait(heard.at[1], len(along_z))
    send(0, SPACE)
    send(1, SPACE + PLANES)
    fill_swap(swap)
    fill_ones(ones)
    local[0].wait()
    fill_bias(rel, strip, bias)
    for copy in local[1:]:
        copy.wait()

    def attention(c):
        here = tokens.at[c]
        pltpu.make_async_copy(here, here, in_sem.at[c]).wait()
        project(0, TILES, here, gain_attn[...][None], w_qkv, swap, qkv)
        if not isinstance(c, int):

            @pl.when(c < CHUNKS - 2)
            def _():
                send(c + 2, SPACE + PLANES)

        @pl.loop(0, CHUNK, unroll=True)
        def _(b):
            attend(b, qkv, bias, ones, mix)

    def rest(c, first, tiles):
        finish(
            first, tiles, tokens.at[c], mix, swap, w_proj, gain_mlp[...][None], w_up, w_down, done.at[c]
        )

    @pl.loop(0, CHUNKS - 1)
    def _(c):
        attention(c)
        rest(c, 0, TILES)
        send_back(c, ORDER)
        keep(c)

    last = CHUNKS - 1
    attention(last)
    rest(last, (1 - z_lo) * 2, 2)
    send_back(last, [d for d in ORDER if d[2] % 2 == 1])
    rest(last, z_lo * 2, 2)
    send_back(last, [d for d in ORDER if d[2] % 2 == 0])
    keep(last)

    pltpu.make_async_copy(out_ref, out_ref, out_sem.at[0]).wait()
    others = x_ref.at[pl.ds(0, MEMBERS - 1)]
    pltpu.make_async_copy(others, others, sent_sem.at[0]).wait()
    pltpu.make_async_copy(others, others, back_sem.at[0]).wait()


def move(src, dst, sems):
    parts = sems.shape[0]
    step = src.shape[0] // parts
    copies = [
        pltpu.make_async_copy(src.at[pl.ds(i * step, step)], dst.at[pl.ds(i * step, step)], sems.at[i])
        for i in range(parts)
    ]
    for copy in copies:
        copy.start()
    for copy in copies:
        copy.wait()


def on_device(tokens_map, gain_attn, w_qkv, w_proj, rel_bias, gain_mlp, w_up, w_down):
    hbm = pl.BlockSpec(memory_space=pltpu.HBM)
    arrived = pl.pallas_call(
        kernel,
        name="grid_block",
        out_shape=pltpu.VMEM(tokens_map.shape, bf16),
        in_specs=[hbm] * 8,
        out_specs=pl.BlockSpec(memory_space=pl.ANY),
        scratch_shapes=[
            pltpu.VMEM((CHUNKS, MEMBERS, CHUNK, D), bf16),
            pltpu.VMEM((CHUNKS, MEMBERS, CHUNK, D), bf16),
            pltpu.VMEM((D,), f32),
            pltpu.VMEM((D,), f32),
            pltpu.VMEM((HEADS, 15, 15), f32),
            pltpu.VMEM((D, 3 * D), bf16),
            pltpu.VMEM((D, D), bf16),
            pltpu.VMEM((D, MLP_DIM), bf16),
            pltpu.VMEM((MLP_DIM, D), bf16),
            pltpu.VMEM((3, CHUNK, MEMBERS, D), bf16),
            pltpu.VMEM((MEMBERS // TILE, CHUNK, TILE, D), bf16),
            pltpu.VMEM((3, MEMBERS, 4 * MEMBERS), f32),
            pltpu.VMEM((HEADS, GRID, 128), f32),
            pltpu.VMEM((256, 256), bf16),
            pltpu.VMEM((256, 128), bf16),
            pltpu.SemaphoreType.REGULAR((2,)),
            pltpu.SemaphoreType.DMA((7,)),
            pltpu.SemaphoreType.DMA((CHUNKS,)),
            pltpu.SemaphoreType.DMA((1,)),
            pltpu.SemaphoreType.DMA((1,)),
            pltpu.SemaphoreType.DMA((1,)),
        ],
        compiler_params=pltpu.CompilerParams(
            collective_id=0, has_side_effects=True, vmem_limit_bytes=44 * 2**20
        ),
    )(*(pltpu.with_memory_space_constraint(a, pltpu.HBM) for a in (tokens_map, gain_attn, w_qkv, w_proj, rel_bias, gain_mlp, w_up, w_down)))
    return pl.pallas_call(
        move,
        name="move_out",
        out_shape=jax.ShapeDtypeStruct(tokens_map.shape, bf16),
        in_specs=[pl.BlockSpec(memory_space=pl.ANY)],
        out_specs=hbm,
        scratch_shapes=[pltpu.SemaphoreType.DMA((2,))],
        compiler_params=pltpu.CompilerParams(vmem_limit_bytes=16 * 2**20),
    )(arrived)


def solution(mesh):
    placed = (P("row", "col", None), P(), P(), P(), P(), P(), P(), P())
    return jax.shard_map(
        on_device, mesh=mesh, in_specs=placed, out_specs=P("row", "col", None), check_vma=False
    )
```

```python
import math

import jax
import jax.numpy as jnp
from jax import lax
from jax.experimental import pallas as pl
from jax.experimental.pallas import tpu as pltpu
from jax.sharding import PartitionSpec as P

MESH = pl.DeviceIdType.MESH
f32, bf16 = jnp.float32, jnp.bfloat16

D = 384
HEADS = 12
HEAD_DIM = 32
MLP_DIM = 1536
GRID = 8
MEMBERS = GRID * GRID
EPSILON = 1e-5
LOG2E = math.log2(math.e)

CHUNK = 16
TILE = 16
CHUNKS = 4
TILES = MEMBERS // TILE


def displacements():
    def hops(d):
        return sum(min(v, 4 - v) for v in d)

    order = []
    for d in sorted(((x, y, z) for x in range(4) for y in range(4) for z in range(4)), key=hops):
        group = []
        for base in (d, tuple((4 - v) % 4 for v in d)):
            group += [base[k:] + base[:k] for k in range(3)]
        if d != (0, 0, 0) and d not in sum(order, []):
            order.append(list(dict.fromkeys(group)))
    return sum(reversed(order), [])


ORDER = displacements()
MIXED = [d for pair in zip(ORDER, ORDER[::-1]) for d in pair][:len(ORDER)]
LINES, PLANES, SPACE = ([d for d in ORDER if d.count(0) == 3 - n] for n in (1, 2, 3))


def norm(values, gain):
    average = jnp.mean(values, -1, keepdims=True)
    centered = values - average
    variance = jnp.mean(centered * centered, -1, keepdims=True)
    return (centered * lax.rsqrt(variance + EPSILON) * gain).astype(bf16)


def fill_swap(swap):
    r = lax.broadcasted_iota(jnp.int32, (256, 256), 0)
    c = lax.broadcasted_iota(jnp.int32, (256, 256), 1)
    swap[...] = ((r // 16 == c % 16) & (r % 16 == c // 16)).astype(bf16)


def fill_ones(ones):
    r = lax.broadcasted_iota(jnp.int32, (256, 128), 0)
    c = lax.broadcasted_iota(jnp.int32, (256, 128), 1)
    ones[...] = (r // MEMBERS == c // HEAD_DIM).astype(bf16)


def fill_bias(rel, strip, bias):
    s = lax.broadcasted_iota(jnp.int32, (15, 1024), 0)
    lane = lax.broadcasted_iota(jnp.int32, (15, 1024), 1)
    g2i, q, g2j = lane // 128, (lane % 128) // 8, lane % 8
    hits = ((s == g2i - g2j + 7) & (q < 15)).astype(f32)
    rows = s == 14 - q
    for h in range(HEADS):
        spread = jnp.dot(rel[h], hits, preferred_element_type=f32, precision=lax.Precision.HIGHEST)
        line = jnp.sum(jnp.where(rows, spread, 0.0), 0, keepdims=True) * LOG2E
        for g in range(GRID):
            strip[h, g:g + 1, :] = line[:, g * 128:(g + 1) * 128]
    for h in range(HEADS):
        u = strip[h]
        for g1 in range(GRID):
            at = (GRID - 1 - g1) * GRID
            lanes = slice((h % 4) * MEMBERS, (h % 4 + 1) * MEMBERS)
            bias[h // 4, g1 * GRID:(g1 + 1) * GRID, lanes] = u[:, at:at + MEMBERS]


def turn(swap, rows):
    parts = [
        jnp.dot(swap, rows[at:at + 256], preferred_element_type=f32).astype(bf16)
        for at in range(0, rows.shape[0], 256)
    ]
    return parts[0] if len(parts) == 1 else jnp.concatenate(parts, 0)


def project(first, tiles, tokens, gain, w_qkv, swap, qkv):
    x = tokens[pl.ds(first, tiles * TILE)].reshape(tiles * 256, D).astype(f32)
    turned = turn(swap[...], norm(x, gain))
    packed = jnp.dot(turned, w_qkv[...], preferred_element_type=f32).astype(bf16)
    for part in range(3):
        for t in range(tiles):
            block = packed[t * 256:(t + 1) * 256, part * D:(part + 1) * D]
            qkv[part, :, pl.ds(first + t * TILE, TILE), :] = block.reshape(CHUNK, TILE, D)


def attend(b, qkv, bias, ones, mix):
    lane = lax.broadcasted_iota(jnp.int32, (1, 128), 1)
    low = lane < MEMBERS
    masks = [(lane // HEAD_DIM == h).astype(bf16) for h in range(4)]
    for hb in range(3):
        cols = slice(hb * 128, (hb + 1) * 128)
        q = qkv[0, b, :, cols]
        k = qkv[1, b, :, cols]
        v = qkv[2, b, :, cols]
        keys = jnp.concatenate([k * m for m in masks], 0)
        values = jnp.concatenate([v * m for m in masks], 0)
        scores = lax.dot_general(q, keys, (((1,), (1,)), ((), ())), preferred_element_type=f32)
        scores = scores * (HEAD_DIM ** -0.5 * LOG2E) + bias[hb]
        weights = []
        for pair in range(2):
            s = scores[:, pair * 128:(pair + 1) * 128]
            peak0 = jnp.max(jnp.where(low, s, -jnp.inf), -1, keepdims=True)
            peak1 = jnp.max(jnp.where(low, -jnp.inf, s), -1, keepdims=True)
            weights.append(jnp.exp2(s - jnp.where(low, peak0, peak1)).astype(bf16))
        sums = jnp.dot(
            jnp.concatenate(weights, 1),
            jnp.concatenate([values, ones[...]], 1),
            preferred_element_type=f32,
        )
        mixture = (sums[:, :128] / sums[:, 128:]).astype(bf16)
        mix[:, pl.ds(b, 1), :, cols] = mixture.reshape(MEMBERS // TILE, 1, TILE, 128)


def finish(first, tiles, tokens, mix, swap, w_proj, gain, w_up, w_down, done):
    rows = tiles * 256
    x = tokens[pl.ds(first * TILE, tiles * TILE)].reshape(rows, D).astype(f32)
    mixture = turn(swap[...], mix[pl.ds(first, tiles)].reshape(rows, D))
    attended = (x + jnp.dot(mixture, w_proj[...], preferred_element_type=f32)).astype(bf16)
    normed = norm(attended.astype(f32), gain)
    hidden = []
    for c in range(0, MLP_DIM, 512):
        u = jnp.dot(normed, w_up[:, c:c + 512], preferred_element_type=f32)
        hidden.append((u * (0.5 * lax.erf(u * (2 ** -0.5)) + 0.5)).astype(bf16))
    total = attended.astype(f32) + jnp.dot(
        jnp.concatenate(hidden, 1), w_down[...], preferred_element_type=f32
    )
    done[pl.ds(first * TILE, tiles * TILE)] = total.astype(bf16).reshape(tiles * TILE, CHUNK, D)


def kernel(
    x_ref, ga_ref, wq_ref, wp_ref, rb_ref, gm_ref, wu_ref, wd_ref,
    out_ref,
    tokens, done, gain_attn, gain_mlp, rel, w_qkv, w_proj, w_up, w_down, qkv, mix, bias, strip, swap, ones,
    heard, weight_sem, in_sem, sent_sem, back_sem, out_sem,
):
    g1 = lax.axis_index("row")
    col = lax.axis_index("col")
    g2, core = lax.div(col, 2), lax.rem(col, 2)
    me = g1 * GRID + g2
    z_lo, x = lax.div(g1, 4), lax.rem(g1, 4)
    y, z = lax.div(g2, 2), lax.rem(g2, 2) * 2 + z_lo
    xs, ys, zs = ([lax.rem(v + k, 4) for k in range(4)] for v in (x, y, z))
    z_highs = [lax.div(v, 2) for v in zs]
    z_lows = [lax.rem(v, 2) for v in zs]

    def partner(d):
        p1 = z_lows[d[2]] * 4 + xs[d[0]]
        p2 = ys[d[1]] * 2 + z_highs[d[2]]
        return p1 * GRID + p2, (p1, p2 * 2 + core)

    barrier = pltpu.get_barrier_semaphore()
    for d in LINES:
        pl.semaphore_signal(barrier, inc=1, device_id=partner(d)[1], device_id_type=MESH)

    local = [
        pltpu.make_async_copy(src, dst, weight_sem.at[i])
        for i, (src, dst) in enumerate((
            (rb_ref, rel), (ga_ref, gain_attn), (wq_ref, w_qkv), (wp_ref, w_proj),
            (gm_ref, gain_mlp), (wu_ref, w_up), (wd_ref, w_down),
        ))
    ]
    for copy in local:
        copy.start()
    for c in range(CHUNKS):
        pltpu.make_async_copy(
            x_ref.at[me, pl.ds(c * CHUNK, CHUNK)], tokens.at[c, me], in_sem.at[c]
        ).start()

    def send(c, order):
        for d in order:
            peer, device = partner(d)
            pltpu.make_async_remote_copy(
                src_ref=x_ref.at[peer, pl.ds(c * CHUNK, CHUNK)],
                dst_ref=tokens.at[c, me],
                send_sem=sent_sem.at[0],
                recv_sem=in_sem.at[c],
                device_id=device,
                device_id_type=MESH,
            ).start()

    def send_back(c, order):
        for d in order:
            peer, device = partner(d)
            pltpu.make_async_remote_copy(
                src_ref=done.at[c, peer],
                dst_ref=out_ref.at[me, pl.ds(c * CHUNK, CHUNK)],
                send_sem=back_sem.at[0],
                recv_sem=out_sem.at[0],
                device_id=device,
                device_id_type=MESH,
            ).start()

    def keep(c):
        pltpu.make_async_copy(
            done.at[c, me], out_ref.at[me, pl.ds(c * CHUNK, CHUNK)], out_sem.at[0]
        ).start()

    def tell(round_, mates):
        for d in mates:
            pl.semaphore_signal(
                heard.at[round_], inc=1, device_id=partner(d)[1], device_id_type=MESH
            )

    along_z = [d for d in LINES if d[2]]
    across = [d for d in LINES if not d[2]]
    pl.semaphore_wait(barrier, len(LINES))
    tell(0, across)
    for c in range(CHUNKS):
        send(c, LINES)
    pl.semaphore_wait(heard.at[0], len(across))
    tell(1, along_z)
    send(0, PLANES)
    pl.semaphore_wait(heard.at[1], len(along_z))
    send(0, SPACE)
    send(1, SPACE + PLANES)
    fill_swap(swap)
    fill_ones(ones)
    local[0].wait()
    fill_bias(rel, strip, bias)
    for copy in local[1:]:
        copy.wait()

    def attention(c):
        here = tokens.at[c]
        pltpu.make_async_copy(here, here, in_sem.at[c]).wait()
        project(0, TILES, here, gain_attn[...][None], w_qkv, swap, qkv)
        if not isinstance(c, int):

            @pl.when(c < CHUNKS - 2)
            def _():
                send(c + 2, SPACE + PLANES)

        @pl.loop(0, CHUNK, unroll=True)
        def _(b):
            attend(b, qkv, bias, ones, mix)

    def rest(c, first, tiles):
        finish(
            first, tiles, tokens.at[c], mix, swap, w_proj, gain_mlp[...][None], w_up, w_down, done.at[c]
        )

    @pl.loop(0, CHUNKS - 1)
    def _(c):
        attention(c)
        rest(c, 0, TILES)
        send_back(c, MIXED)
        keep(c)

    last = CHUNKS - 1
    attention(last)
    rest(last, (1 - z_lo) * 2, 2)
    send_back(last, [d for d in ORDER if d[2] % 2 == 1])
    rest(last, z_lo * 2, 2)
    send_back(last, [d for d in ORDER if d[2] % 2 == 0])
    keep(last)

    pltpu.make_async_copy(out_ref, out_ref, out_sem.at[0]).wait()
    others = x_ref.at[pl.ds(0, MEMBERS - 1)]
    pltpu.make_async_copy(others, others, sent_sem.at[0]).wait()
    pltpu.make_async_copy(others, others, back_sem.at[0]).wait()


def move(src, dst, sems):
    parts = sems.shape[0]
    step = src.shape[0] // parts
    copies = [
        pltpu.make_async_copy(src.at[pl.ds(i * step, step)], dst.at[pl.ds(i * step, step)], sems.at[i])
        for i in range(parts)
    ]
    for copy in copies:
        copy.start()
    for copy in copies:
        copy.wait()


def on_device(tokens_map, gain_attn, w_qkv, w_proj, rel_bias, gain_mlp, w_up, w_down):
    hbm = pl.BlockSpec(memory_space=pltpu.HBM)
    arrived = pl.pallas_call(
        kernel,
        name="grid_block",
        out_shape=pltpu.VMEM(tokens_map.shape, bf16),
        in_specs=[hbm] * 8,
        out_specs=pl.BlockSpec(memory_space=pl.ANY),
        scratch_shapes=[
            pltpu.VMEM((CHUNKS, MEMBERS, CHUNK, D), bf16),
            pltpu.VMEM((CHUNKS, MEMBERS, CHUNK, D), bf16),
            pltpu.VMEM((D,), f32),
            pltpu.VMEM((D,), f32),
            pltpu.VMEM((HEADS, 15, 15), f32),
            pltpu.VMEM((D, 3 * D), bf16),
            pltpu.VMEM((D, D), bf16),
            pltpu.VMEM((D, MLP_DIM), bf16),
            pltpu.VMEM((MLP_DIM, D), bf16),
            pltpu.VMEM((3, CHUNK, MEMBERS, D), bf16),
            pltpu.VMEM((MEMBERS // TILE, CHUNK, TILE, D), bf16),
            pltpu.VMEM((3, MEMBERS, 4 * MEMBERS), f32),
            pltpu.VMEM((HEADS, GRID, 128), f32),
            pltpu.VMEM((256, 256), bf16),
            pltpu.VMEM((256, 128), bf16),
            pltpu.SemaphoreType.REGULAR((2,)),
            pltpu.SemaphoreType.DMA((7,)),
            pltpu.SemaphoreType.DMA((CHUNKS,)),
            pltpu.SemaphoreType.DMA((1,)),
            pltpu.SemaphoreType.DMA((1,)),
            pltpu.SemaphoreType.DMA((1,)),
        ],
        compiler_params=pltpu.CompilerParams(
            collective_id=0, has_side_effects=True, vmem_limit_bytes=44 * 2**20
        ),
    )(*(pltpu.with_memory_space_constraint(a, pltpu.HBM) for a in (tokens_map, gain_attn, w_qkv, w_proj, rel_bias, gain_mlp, w_up, w_down)))
    return pl.pallas_call(
        move,
        name="move_out",
        out_shape=jax.ShapeDtypeStruct(tokens_map.shape, bf16),
        in_specs=[pl.BlockSpec(memory_space=pl.ANY)],
        out_specs=hbm,
        scratch_shapes=[pltpu.SemaphoreType.DMA((2,))],
        compiler_params=pltpu.CompilerParams(vmem_limit_bytes=16 * 2**20),
    )(arrived)


def solution(mesh):
    placed = (P("row", "col", None), P(), P(), P(), P(), P(), P(), P())
    return jax.shard_map(
        on_device, mesh=mesh, in_specs=placed, out_specs=P("row", "col", None), check_vma=False
    )
```
